128 devices in a mesh: fsdp: 32 (over z, x, core), feat: 4 (over y).
Axes of the slice: x: 4, y: 4, z: 4, core: 2. Of those that a mesh axis runs over, the one named last changes fastest.
Arguments:
- table_cells: bfloat16 [1536, 256, 192], P(('fsdp', 'feat'))
- attn_weights: bfloat16 [8, 192, 192], P(None, 'fsdp')
- hidden_up_weight: bfloat16 [192, 384], P('fsdp'), may hold values from -0.4375 to 0.4375
- hidden_down_weight: bfloat16 [384, 192], P('fsdp'), may hold values from -0.3125 to 0.3125
- norm_gains: float32 [3, 192], replicated, may hold values from 0.25 to 1.75
- train_count: int32 [1], replicated, may hold values from 384 to 1152
- feature_count: int32 [1], replicated, may hold values from 128 to 256
Outputs:
- layer_out: bfloat16 [1536, 256, 192], P(('fsdp', 'feat'))
The draws below stay inside these ranges and needn't reach their ends.
Inputs may be any that keep to these rules, and one draw needn't show every extreme that they name: Rows 0 to train_count - 1 are the training rows. Features 0 to feature_count - 1 are real, the others padding.
All inputs are finite; a program needn't handle non-finite values.
Results may differ from the reference program's by a relative error of at most 0.012.
The reference program's roundings to bfloat16 on the way (of `normed_one`, `mixed_rows`, `normed_two`, `sampled` and `activated`) count: a program that leaves them out, or rounds other values in their place, can miss the bound.
Values may be sent and summed in bfloat16 or wider, within the bound.
A program may use at most 128 MiB of HBM per device.

```python
import jax
import jax.numpy as jnp
from jax import lax

D = 192
HEADS = 6
FF = 384
FEATS = 256
ROWS = 1536


def draw_table_cells(key, part):
    key = jax.random.fold_in(key, 11)
    base = jax.random.normal(key, (ROWS, FEATS, D), jnp.float32)
    return base.astype(jnp.bfloat16)


def draw_attn_weights(key, part):
    key = jax.random.fold_in(key, 23)
    spread = D ** (-0.5)
    stack = jax.random.normal(key, (8, D, D), jnp.float32) * spread
    return stack.astype(jnp.bfloat16)


def block_scale(key, extent, cuts, low, top_value):
    def one(dim, shards_of):
        steps = jax.random.uniform(jax.random.fold_in(jax.random.fold_in(key, 6), dim), (shards_of,), jnp.float32, low / len(cuts), top_value / len(cuts))
        return jnp.repeat(jnp.exp(steps), extent[dim] // shards_of).reshape((-1,) + (1,) * (len(extent) - dim - 1))

    factor_of = one(*cuts[0])
    for cut in cuts[1:]:
        factor_of = factor_of * one(*cut)
    return factor_of


def scatter_about(key, shape, scale, limit, cuts=(), kind=jnp.bfloat16):
    array = jax.random.normal(key, shape, jnp.float32) * scale
    if len(cuts) > 0:
        array = block_scale(key, shape, cuts, -0.22, 0.18) * array
    return jnp.clip(array, min=-limit, max=limit).astype(kind)


def setup_inputs(seed: int = 0) -> dict:
    key_of = jax.random.split(jax.random.key(seed), 8)
    table_cells = draw_table_cells(jax.random.fold_in(key_of[7], 71), 0)
    attn_weights = draw_attn_weights(jax.random.fold_in(key_of[7], 71), 0)
    hidden_up_weight = scatter_about(key_of[2], (D, FF), D ** -0.5, 0.4375, ((0, 32),))
    hidden_down_weight = scatter_about(key_of[3], (FF, D), FF ** -0.5, 0.3125, ((0, 32),))
    norm_gains = jnp.clip(1.0 + 0.15 * jax.random.normal(key_of[4], (3, D), jnp.float32), 0.25, 1.75)
    train_count = jax.random.randint(key_of[5], (1,), ROWS // 4, ROWS * 3 // 4 + 1).astype(jnp.int32)
    feature_count = jax.random.randint(key_of[6], (1,), FEATS // 2, FEATS + 1).astype(jnp.int32)
    return dict(table_cells=table_cells, attn_weights=attn_weights, hidden_up_weight=hidden_up_weight, hidden_down_weight=hidden_down_weight, norm_gains=norm_gains, train_count=train_count, feature_count=feature_count)


EPS = 1e-05
NEGATIVE = -1e+30

def normalize(value_rows, gain):
    floats = value_rows.astype(jnp.float32)
    average = lax.optimization_barrier(jnp.mean(floats, axis=-1, keepdims=True))
    centered = floats - average
    variance = lax.optimization_barrier(jnp.mean(centered * centered, axis=-1, keepdims=True))
    return (centered * lax.rsqrt(variance + EPS) * gain).astype(jnp.bfloat16)

def softmax_rows(scores, live):
    masked = jnp.where(live, scores, NEGATIVE)
    row_maximum = lax.optimization_barrier(jnp.max(masked, axis=-1, keepdims=True))
    exponent = jnp.exp(masked - row_maximum)
    return (exponent / lax.optimization_barrier(jnp.sum(exponent, axis=-1, keepdims=True))).astype(jnp.bfloat16)

def attend(normed, weights, live):
    model_width = normed.shape[-1]
    head_size = model_width // HEADS
    queries = jnp.dot(normed, weights[0], preferred_element_type=jnp.float32).astype(jnp.bfloat16)
    keys = jnp.dot(normed, weights[1], preferred_element_type=jnp.float32).astype(jnp.bfloat16)
    value_rows = jnp.dot(normed, weights[2], preferred_element_type=jnp.float32).astype(jnp.bfloat16)
    queries = queries.reshape(-1, HEADS, head_size).astype(jnp.float32)
    keys = keys.reshape(-1, HEADS, head_size).astype(jnp.float32)
    value_rows = value_rows.reshape(-1, HEADS, head_size).astype(jnp.float32)
    scores = jnp.einsum('qhe,khe->hqk', queries, keys) * head_size ** (-0.5)
    attention_probabilities = softmax_rows(scores, live[None, None, :])
    heads_out = jnp.einsum('hqk,khe->qhe', attention_probabilities.astype(jnp.float32), value_rows)
    heads_out = heads_out.astype(jnp.bfloat16).reshape(-1, model_width)
    return jnp.dot(heads_out, weights[3], preferred_element_type=jnp.float32)

def feed_forward(value_rows, gain, w_in, w_out):
    normed = normalize(value_rows, gain)
    hidden = jnp.dot(normed.reshape(-1, D), w_in, preferred_element_type=jnp.float32)
    activated = jax.nn.gelu(hidden).astype(jnp.bfloat16)
    result = value_rows.astype(jnp.float32) + jnp.dot(activated, w_out, preferred_element_type=jnp.float32).reshape(value_rows.shape)
    return result.astype(jnp.bfloat16)

def reference(table_cells, attn_weights, hidden_up_weight, hidden_down_weight, norm_gains, train_count, feature_count):
    feat_live = jnp.arange(FEATS) < feature_count[0]
    row_live = jnp.arange(ROWS) < train_count[0]
    normed_one = normalize(table_cells, norm_gains[0])

    def by_row(pair):
        row_cells, row_normalized = pair
        return (row_cells.astype(jnp.float32) + attend(row_normalized, attn_weights[0:4], feat_live)).astype(jnp.bfloat16)
    mixed_rows = lax.map(by_row, (table_cells, normed_one))
    columns = jnp.swapaxes(mixed_rows, 0, 1)
    normed_two = normalize(columns, norm_gains[1])

    def by_feature(pair):
        col_cells, col_normed = pair
        return (col_cells.astype(jnp.float32) + attend(col_normed, attn_weights[4:8], row_live)).astype(jnp.bfloat16)
    sampled = jnp.swapaxes(lax.map(by_feature, (columns, normed_two)), 0, 1)
    return feed_forward(sampled, norm_gains[2], hidden_up_weight, hidden_down_weight)
```

```python
import functools

import jax
import jax.numpy as jnp
from jax import lax
from jax.experimental import pallas as pl
from jax.experimental.pallas import tpu as pltpu
from jax.sharding import PartitionSpec as P

MESH = pl.DeviceIdType.MESH
HEADS = 6
EPS = 1e-05
NEGATIVE = -1e30
EXT = 48
MSG = 40
F32 = jnp.float32
BF16 = jnp.bfloat16
VMEM = pl.BlockSpec(memory_space=pltpu.VMEM)
SMEM = pl.BlockSpec(memory_space=pltpu.SMEM)


def norm_t(cells_t, gain):
    mean = jnp.mean(cells_t, axis=0, keepdims=True)
    centered = cells_t - mean
    var = jnp.mean(centered * centered, axis=0, keepdims=True)
    return (centered * lax.rsqrt(var + EPS) * gain).astype(BF16)


def dot(a, b):
    return jnp.dot(a, b, preferred_element_type=F32)


def first_row(count, top):
    rows = lax.broadcasted_iota(jnp.int32, (16, count), 0)
    return jnp.where(rows == 0, top, 0.0).astype(F32)


def wait_all(ref, count, sem):
    blocks = ref.at[pl.ds(0, count)]
    pltpu.make_async_copy(blocks, blocks, sem).wait()


def gather_kernel(n, shard_ref, full_ref, send, recv, own_sem):
    me, feat = lax.axis_index("fsdp"), lax.axis_index("feat")
    barrier = pltpu.get_barrier_semaphore()

    @pl.loop(1, n)
    def _(k):
        pl.semaphore_signal(
            barrier, inc=1, device_id=(lax.rem(me + k, n), feat), device_id_type=MESH
        )

    own = pltpu.make_async_copy(shard_ref, full_ref.at[me], own_sem)
    own.start()
    pl.semaphore_wait(barrier, n - 1)

    def copy(k):
        return pltpu.make_async_remote_copy(
            src_ref=shard_ref,
            dst_ref=full_ref.at[me],
            send_sem=send,
            recv_sem=recv,
            device_id=(lax.rem(me + k, n), feat),
            device_id_type=MESH,
        )

    @pl.loop(1, n)
    def _(k):
        copy(k).start()

    own.wait()
    wait_all(full_ref, n - 1, send)
    wait_all(full_ref, n - 1, recv)


def gather(shard, n):
    return pl.pallas_call(
        functools.partial(gather_kernel, n),
        out_shape=jax.ShapeDtypeStruct((n,) + shard.shape, shard.dtype),
        in_specs=[VMEM],
        out_specs=VMEM,
        scratch_shapes=[pltpu.SemaphoreType.DMA] * 3,
        compiler_params=pltpu.CompilerParams(
            collective_id=0, has_side_effects=True, vmem_limit_bytes=40 * 2**20
        ),
        name="gather_weights",
    )(shard)


def stack_weights(full_ref, first, last, scratch, out_ref):
    n, rows, _ = full_ref.shape
    for i in range(n):
        scratch[pl.ds(i * rows, rows), :] = full_ref[i, :, first:last].astype(F32)
    for c in range(0, last - first, 128):
        out_ref[c : c + 128, :] = scratch[:, c : c + 128].T.astype(BF16)


def feature_kernel(
    count_ref, x_ref, full_ref, gains_ref, out_ref, w_f32, w_ref, cells
):
    rows, feats, width = x_ref.shape
    head = width // HEADS
    scale = head**-0.5 * 1.4426950408889634
    stack_weights(full_ref, 0, 4 * width, w_f32, w_ref)
    live = lax.broadcasted_iota(jnp.int32, (1, feats), 1) < count_ref[0]
    mask = first_row(feats, jnp.where(live, 0.0, NEGATIVE))
    ones = first_row(feats, 1.0)
    ones_b = ones.astype(BF16)
    gain = gains_ref[:, 0:1]

    def row(r, carry):
        x_t = x_ref[r].astype(F32).T
        normed = norm_t(x_t, gain)
        qkv = dot(w_ref[0 : 3 * width, :], normed)
        heads = []
        for h in range(HEADS):
            q = (qkv[h * head : (h + 1) * head] * scale).astype(BF16)
            q = jnp.concatenate([q, ones_b], axis=0)
            k = jnp.concatenate([qkv[width + h * head : width + (h + 1) * head], mask], axis=0)
            k = k.T.astype(BF16)
            v = qkv[2 * width + h * head : 2 * width + (h + 1) * head].astype(BF16)
            v = jnp.concatenate([v, ones_b], axis=0)
            s = dot(k, q)
            p = jnp.exp2(s - jnp.max(s, axis=0, keepdims=True)).astype(BF16)
            o = dot(v, p)
            heads.append((o[:head] / o[head : head + 1]).astype(BF16))
        y = dot(w_ref[3 * width : 4 * width, :], jnp.concatenate(heads, axis=0)) + x_t
        half = feats // 2
        y = jnp.concatenate([y[:, :half], y[:, half:]], axis=0)
        for t in range(3):
            cells[pl.ds(t * rows + r, half, stride=MSG), :] = y[t * 128 : (t + 1) * 128].T
        return carry

    lax.fori_loop(0, rows, row, 0)

    def pack(d, carry):
        at = pl.multiple_of(d * MSG, 8)
        out_ref[d] = cells[pl.ds(at, MSG), :].astype(BF16)
        return carry

    lax.fori_loop(0, feats // 2, pack, 0, unroll=4)


def feature_part(count, x, full, gains_t, devices):
    rows, feats, width = x.shape
    return pl.pallas_call(
        feature_kernel,
        out_shape=jax.ShapeDtypeStruct((devices, MSG, 128), BF16),
        in_specs=[SMEM, VMEM, VMEM, VMEM],
        out_specs=VMEM,
        scratch_shapes=[
            pltpu.VMEM((width, 4 * width), F32),
            pltpu.VMEM((4 * width, width), BF16),
            pltpu.VMEM((devices * MSG, 128), F32),
        ],
        compiler_params=pltpu.CompilerParams(vmem_limit_bytes=50 * 2**20),
        name="feature_attention",
    )(count, x, full, gains_t)


def position(fsdp, feat, k, groups, devices):
    d = lax.rem(fsdp * groups + feat + k, devices)
    return d // groups, lax.rem(d, groups)


def exchange(groups, devices, src_ref, dst_ref, send, recv, own_sem):
    fsdp, feat = lax.axis_index("fsdp"), lax.axis_index("feat")
    me = fsdp * groups + feat
    barrier = pltpu.get_barrier_semaphore()

    @pl.loop(1, devices)
    def _(k):
        pl.semaphore_signal(
            barrier, inc=1, device_id=position(fsdp, feat, k, groups, devices), device_id_type=MESH
        )

    own = pltpu.make_async_copy(src_ref.at[me], dst_ref.at[me], own_sem)
    own.start()
    pl.semaphore_wait(barrier, devices - 1)

    def copy(k):
        to = position(fsdp, feat, k, groups, devices)
        return pltpu.make_async_remote_copy(
            src_ref=src_ref.at[to[0] * groups + to[1]],
            dst_ref=dst_ref.at[me],
            send_sem=send,
            recv_sem=recv,
            device_id=to,
            device_id_type=MESH,
        )

    @pl.loop(1, devices)
    def _(k):
        copy(k).start()

    own.wait()
    wait_all(dst_ref, devices - 1, send)
    wait_all(dst_ref, devices - 1, recv)


def all_to_all(messages, groups):
    return pl.pallas_call(
        functools.partial(exchange, groups, messages.shape[0]),
        out_shape=jax.ShapeDtypeStruct(messages.shape, messages.dtype),
        in_specs=[VMEM],
        out_specs=VMEM,
        scratch_shapes=[pltpu.SemaphoreType.DMA] * 3,
        compiler_params=pltpu.CompilerParams(
            collective_id=1, has_side_effects=True, vmem_limit_bytes=40 * 2**20
        ),
        name="to_columns",
    )(messages)


def sample_kernel(
    block_q, block_k, count_ref, in_ref, full_ref, gains_ref, out_ref,
    w_f32, w_ref, cells, x_t, q_all, k_all, v_all, acc, top, out_t,
):
    devices = in_ref.shape[0]
    total = cells.shape[1]
    rows = total // devices
    width = gains_ref.shape[0]
    head = width // HEADS
    scale = head**-0.5 * 1.4426950408889634
    stack_weights(full_ref, 4 * width, 12 * width, w_f32, w_ref)

    def unpack(i, carry):
        for j in range(2):
            block = in_ref[2 * i + j].astype(F32)
            at = pl.multiple_of(i * 2 * rows, 8)
            for t in range(3):
                cells[t, pl.ds(at + j * rows, rows), :] = block[t * rows : (t + 1) * rows]
        return carry

    lax.fori_loop(0, devices // 2, unpack, 0, unroll=2)
    for t in range(3):
        for c in range(0, total, 128):
            x_t[t * 128 : (t + 1) * 128, c : c + 128] = cells[t, c : c + 128, :].T
    gain2, gain3 = gains_ref[:, 1:2], gains_ref[:, 2:3]
    ones = first_row(block_q, 1.0).astype(BF16)
    live_blocks = lax.div(count_ref[0] + (block_k - 1), block_k)

    for f in range(2):
        base = f * width

        def project(b, carry):
            at = pl.multiple_of(b * block_q, 128)
            lanes = pl.ds(at, block_q)
            normed = norm_t(x_t[base : base + width, lanes], gain2)
            qkv = dot(w_ref[0 : 3 * width, :], normed)
            live = lax.broadcasted_iota(jnp.int32, (1, block_q), 1) + at < count_ref[0]
            mask = first_row(block_q, jnp.where(live, 0.0, NEGATIVE))
            for h in range(HEADS):
                q = (qkv[h * head : (h + 1) * head] * scale).astype(BF16)
                q_all[h, :, lanes] = jnp.concatenate([q, ones], axis=0)
                k = jnp.concatenate([qkv[width + h * head : width + (h + 1) * head], mask], axis=0)
                k_all[h, lanes, :] = k.T.astype(BF16)
                v = qkv[2 * width + h * head : 2 * width + (h + 1) * head].astype(BF16)
                v_all[h, :, lanes] = jnp.concatenate([v, ones], axis=0)
            return carry

        lax.fori_loop(0, total // block_q, project, 0)

        def queries(b, carry):
            lanes = pl.ds(pl.multiple_of(b * block_q, 128), block_q)
            acc[...] = jnp.zeros_like(acc)
            top[...] = jnp.full_like(top, NEGATIVE)

            def keys(j, inner):
                span = pl.ds(pl.multiple_of(j * block_k, 128), block_k)
                for h in range(HEADS):
                    s = dot(k_all[h, span, :], q_all[h, :, lanes])
                    before = top[h : h + 1]
                    now = jnp.maximum(before, jnp.max(s, axis=0, keepdims=True))
                    p = jnp.exp2(s - now).astype(BF16)
                    top[h : h + 1] = now
                    acc[h] = acc[h] * jnp.exp2(before - now) + dot(v_all[h, :, span], p)
                return inner

            lax.fori_loop(0, live_blocks, keys, 0)
            heads = [(acc[h, :head] / acc[h, head : head + 1]).astype(BF16) for h in range(HEADS)]
            y = dot(w_ref[3 * width : 4 * width, :], jnp.concatenate(heads, axis=0))
            sampled = (y + x_t[base : base + width, lanes]).astype(BF16).astype(F32)
            normed = norm_t(sampled, gain3)
            hidden = jax.nn.gelu(dot(w_ref[4 * width : 6 * width, :], normed)).astype(BF16)
            y = dot(w_ref[6 * width : 7 * width, :], hidden[:width])
            y += dot(w_ref[7 * width : 8 * width, :], hidden[width:])
            out_t[base : base + width, lanes] = sampled + y
            return carry

        lax.fori_loop(0, total // block_q, queries, 0)

    for t in range(3):
        for c in range(0, total, 128):
            cells[t, c : c + 128, :] = out_t[t * 128 : (t + 1) * 128, c : c + 128].T

    def pack(i, carry):
        for j in range(2):
            at = pl.multiple_of(i * 2 * rows, 8)
            for t in range(3):
                out_ref[2 * i + j, t * rows : (t + 1) * rows, :] = cells[
                    t, pl.ds(at + j * rows, rows), :
                ].astype(BF16)
        return carry

    lax.fori_loop(0, devices // 2, pack, 0, unroll=2)


def sample_part(count, columns, full, gains_t, total):
    width = gains_t.shape[0]
    block_q, block_k = 512, 128
    return pl.pallas_call(
        functools.partial(sample_kernel, block_q, block_k),
        out_shape=jax.ShapeDtypeStruct(columns.shape, BF16),
        in_specs=[SMEM, VMEM, VMEM, VMEM],
        out_specs=VMEM,
        scratch_shapes=[
            pltpu.VMEM((width, 8 * width), F32),
            pltpu.VMEM((8 * width, width), BF16),
            pltpu.VMEM((3, total, 128), F32),
            pltpu.VMEM((2 * width, total), F32),
            pltpu.VMEM((HEADS, EXT, total), BF16),
            pltpu.VMEM((HEADS, total, EXT), BF16),
            pltpu.VMEM((HEADS, EXT, total), BF16),
            pltpu.VMEM((HEADS, EXT, block_q), F32),
            pltpu.VMEM((8, block_q), F32),
            pltpu.VMEM((2 * width, total), F32),
        ],
        compiler_params=pltpu.CompilerParams(vmem_limit_bytes=56 * 2**20),
        name="sample_attention",
    )(count, columns, full, gains_t)


def back_kernel(groups, devices, src_ref, out_ref, landed, cells, send, recv, own_sem):
    rows, feats, width = out_ref.shape
    half = feats // 2
    exchange(groups, devices, src_ref, landed, send, recv, own_sem)

    def unpack(d, carry):
        cells[pl.ds(pl.multiple_of(d * MSG, 8), MSG), :] = landed[d].astype(F32)
        return carry

    lax.fori_loop(0, devices, unpack, 0, unroll=4)

    def row(r, carry):
        a, b, c = (cells[pl.ds(t * rows + r, half, stride=MSG), :] for t in range(3))
        out_ref[r, :half, :128] = a.astype(BF16)
        out_ref[r, :half, 128:] = b[:, :64].astype(BF16)
        out_ref[r, half:, :] = jnp.concatenate([b[:, 64:], c], axis=1).astype(BF16)
        return carry

    lax.fori_loop(0, rows, row, 0)


def back_to_rows(messages, groups, shape):
    devices = messages.shape[0]
    return pl.pallas_call(
        functools.partial(back_kernel, groups, devices),
        out_shape=jax.ShapeDtypeStruct(shape, BF16),
        in_specs=[VMEM],
        out_specs=VMEM,
        scratch_shapes=[
            pltpu.VMEM(messages.shape, BF16),
            pltpu.VMEM((devices * MSG, 128), F32),
            *[pltpu.SemaphoreType.DMA] * 3,
        ],
        compiler_params=pltpu.CompilerParams(
            collective_id=2, has_side_effects=True, vmem_limit_bytes=40 * 2**20
        ),
        name="back_to_rows",
    )(messages)


def local(table_cells, attn, up, down, norm_gains, train_count, feature_count):
    rows, feats, width = table_cells.shape
    n, groups = lax.axis_size("fsdp"), lax.axis_size("feat")
    devices = n * groups
    part = width // n
    shard = jnp.concatenate(
        [
            jnp.swapaxes(attn, 0, 1).reshape(part, 8 * width),
            jnp.swapaxes(up.reshape(part, width, 2), 1, 2).reshape(part, 2 * width),
            down.reshape(part, 2 * width),
        ],
        axis=1,
    )
    full = gather(shard, n)
    gains_t = norm_gains.T
    messages = feature_part(feature_count, table_cells, full, gains_t, devices)
    columns = all_to_all(messages, groups)
    done = sample_part(train_count, columns, full, gains_t, rows * devices)
    return back_to_rows(done, groups, table_cells.shape)


def solution(mesh):
    in_specs = (
        P(("fsdp", "feat"), None, None),
        P(None, "fsdp", None),
        P("fsdp", None),
        P("fsdp", None),
        P(),
        P(),
        P(),
    )
    out_specs = P(("fsdp", "feat"), None, None)
    return jax.shard_map(local, mesh=mesh, in_specs=in_specs, out_specs=out_specs, check_vma=False)
```

```python
import functools

import jax
import jax.numpy as jnp
from jax import lax
from jax.experimental import pallas as pl
from jax.experimental.pallas import tpu as pltpu
from jax.sharding import PartitionSpec as P

MESH = pl.DeviceIdType.MESH
HEADS = 6
EPS = 1e-05
NEGATIVE = -1e30
EXT = 48
MSG = 40
EARLY = 8
F32 = jnp.float32
BF16 = jnp.bfloat16
VMEM = pl.BlockSpec(memory_space=pltpu.VMEM)
SMEM = pl.BlockSpec(memory_space=pltpu.SMEM)


def norm_t(cells_t, gain):
    mean = jnp.mean(cells_t, axis=0, keepdims=True)
    centered = cells_t - mean
    var = jnp.mean(centered * centered, axis=0, keepdims=True)
    return (centered * lax.rsqrt(var + EPS) * gain).astype(BF16)


def dot(a, b):
    return jnp.dot(a, b, preferred_element_type=F32)


def first_row(count, top):
    rows = lax.broadcasted_iota(jnp.int32, (16, count), 0)
    return jnp.where(rows == 0, top, 0.0).astype(F32)


def wait_all(ref, count, sem):
    blocks = ref.at[pl.ds(0, count)]
    pltpu.make_async_copy(blocks, blocks, sem).wait()


def gather_kernel(n, shard_ref, full_ref, send, recv, own_sem):
    me, feat = lax.axis_index("fsdp"), lax.axis_index("feat")
    barrier = pltpu.get_barrier_semaphore()

    @pl.loop(1, n)
    def _(k):
        pl.semaphore_signal(
            barrier, inc=1, device_id=(lax.rem(me + k, n), feat), device_id_type=MESH
        )

    own = pltpu.make_async_copy(shard_ref, full_ref.at[me], own_sem)
    own.start()
    pl.semaphore_wait(barrier, n - 1)

    def copy(k):
        return pltpu.make_async_remote_copy(
            src_ref=shard_ref,
            dst_ref=full_ref.at[me],
            send_sem=send,
            recv_sem=recv,
            device_id=(lax.rem(me + k, n), feat),
            device_id_type=MESH,
        )

    @pl.loop(1, n)
    def _(k):
        copy(k).start()

    own.wait()
    wait_all(full_ref, n - 1, send)
    wait_all(full_ref, n - 1, recv)


def gather(shard, n):
    return pl.pallas_call(
        functools.partial(gather_kernel, n),
        out_shape=jax.ShapeDtypeStruct((n,) + shard.shape, shard.dtype),
        in_specs=[VMEM],
        out_specs=VMEM,
        scratch_shapes=[pltpu.SemaphoreType.DMA] * 3,
        compiler_params=pltpu.CompilerParams(
            collective_id=0, has_side_effects=True, vmem_limit_bytes=40 * 2**20
        ),
        name="gather_weights",
    )(shard)


def stack_weights(full_ref, first, last, scratch, out_ref, between=None):
    n, rows, _ = full_ref.shape
    for i in range(n):
        scratch[pl.ds(i * rows, rows), :] = full_ref[i, :, first:last].astype(F32)
        if between is not None:
            between(i)
    for c in range(0, last - first, 128):
        out_ref[c : c + 128, :] = scratch[:, c : c + 128].T.astype(BF16)


def position(fsdp, feat, k, groups, devices):
    d = lax.rem(fsdp * groups + feat + k, devices)
    return d // groups, lax.rem(d, groups)


def feature_kernel(
    groups, devices, count_ref, x_ref, full_ref, shard_ref, gains_ref,
    early_ref, late_ref, rest_ref, w_f32, w_ref, cells_a, cells_b, out_a, out_b, send, recv, own,
):
    rows, feats, width = x_ref.shape
    head = width // HEADS
    half = feats // 2
    n = devices // groups
    scale = head**-0.5 * 1.4426950408889634
    fsdp, feat = lax.axis_index("fsdp"), lax.axis_index("feat")
    me = fsdp * groups + feat
    barrier = pltpu.get_barrier_semaphore()
    each = devices // n

    def greet(i):
        for k in range(max(1, i * each), (i + 1) * each):
            pl.semaphore_signal(
                barrier, inc=1, device_id=position(fsdp, feat, k, groups, devices),
                device_id_type=MESH,
            )

    stack_weights(full_ref, 0, 4 * width, w_f32, w_ref, greet)
    live = lax.broadcasted_iota(jnp.int32, (1, feats), 1) < count_ref[0]
    mask = first_row(feats, jnp.where(live, 0.0, NEGATIVE))
    ones_b = first_row(feats, 1.0).astype(BF16)
    gain = gains_ref[:, 0:1]

    def two_rows(i, cells, stride, height, skip):
        x_t = jnp.concatenate([x_ref[2 * i + j].astype(F32).T for j in range(2)], axis=1)
        qkv = dot(w_ref[0 : 3 * width, :], norm_t(x_t, gain))

        def part(unit, kind):
            j, h = unit // HEADS, unit % HEADS
            at = kind * width + h * head
            return qkv[at : at + head, j * feats : (j + 1) * feats]

        def score(unit):
            q = jnp.concatenate([(part(unit, 0) * scale).astype(BF16), ones_b], axis=0)
            k = jnp.concatenate([part(unit, 1), mask], axis=0).T.astype(BF16)
            return dot(k, q)

        heads = []
        s = score(0)
        for unit in range(2 * HEADS):
            following = score(unit + 1) if unit + 1 < 2 * HEADS else None
            p = jnp.exp2(s - jnp.max(s, axis=0, keepdims=True)).astype(BF16)
            o = dot(jnp.concatenate([part(unit, 2).astype(BF16), ones_b], axis=0), p)
            heads.append((o[:head] / o[head : head + 1]).astype(BF16))
            s = following
        heads = jnp.concatenate(
            [jnp.concatenate(heads[:HEADS], axis=0), jnp.concatenate(heads[HEADS:], axis=0)], axis=1
        )
        y = dot(w_ref[3 * width : 4 * width, :], heads) + x_t
        for j in range(2):
            at = j * feats
            m = jnp.concatenate([y[:, at : at + half], y[:, at + half : at + feats]], axis=0)
            for t in range(3):
                cells[pl.ds(t * height + 2 * i + j - skip, half, stride=stride), :] = m[
                    t * 128 : (t + 1) * 128
                ].T

    def send_rest(k):
        pltpu.make_async_remote_copy(
            src_ref=shard_ref, dst_ref=rest_ref.at[fsdp],
            send_sem=send.at[0], recv_sem=recv.at[0],
            device_id=(lax.rem(fsdp + k, n), feat), device_id_type=MESH,
        ).start()

    def send_cells(k, src, dst, which):
        to = position(fsdp, feat, k, groups, devices)
        pltpu.make_async_remote_copy(
            src_ref=src.at[to[0] * groups + to[1]], dst_ref=dst.at[me],
            send_sem=send.at[which], recv_sem=recv.at[which],
            device_id=to, device_id_type=MESH,
        ).start()

    def pack(cells, out, d):
        stride = cells.shape[0] // devices
        at = pl.multiple_of(d * stride, 8)
        out[d] = cells[pl.ds(at, out.shape[1]), :].astype(BF16)

    early = lambda i: two_rows(i, cells_a, 3 * EARLY, EARLY, 0)
    late = lambda i: two_rows(i, cells_b, 16, rows - EARLY, EARLY)

    early(0)
    own_rest = pltpu.make_async_copy(shard_ref, rest_ref.at[fsdp], own.at[0])
    own_rest.start()
    pl.semaphore_wait(barrier, devices - 1)

    @pl.loop(1, n)
    def _(k):
        send_rest(k)

    @pl.loop(1, EARLY // 2)
    def _(i):
        early(i)

    pack(cells_a, out_a, me)
    own_a = pltpu.make_async_copy(out_a.at[me], early_ref.at[me], own.at[1])
    own_a.start()

    @pl.loop(1, devices)
    def _(k):
        pack(cells_a, out_a, lax.rem(me + k, devices))
        send_cells(k, out_a, early_ref, 1)

    @pl.loop(EARLY // 2, rows // 2)
    def _(i):
        late(i)

    pack(cells_b, out_b, me)
    own_b = pltpu.make_async_copy(out_b.at[me], late_ref.at[me], own.at[2])
    own_b.start()

    @pl.loop(1, devices)
    def _(k):
        pack(cells_b, out_b, lax.rem(me + k, devices))
        send_cells(k, out_b, late_ref, 2)

    own_rest.wait()
    own_a.wait()
    own_b.wait()
    for which, ref in enumerate((rest_ref, early_ref, late_ref)):
        wait_all(ref, ref.shape[0] - 1, send.at[which])
        wait_all(ref, ref.shape[0] - 1, recv.at[which])


def feature_part(count, x, full, shard, gains_t, groups, devices):
    rows, feats, width = x.shape
    n = devices // groups
    early, late = (devices, 3 * EARLY, 128), (devices, 3 * (rows - EARLY), 128)
    return pl.pallas_call(
        functools.partial(feature_kernel, groups, devices),
        out_shape=[
            jax.ShapeDtypeStruct(early, BF16),
            jax.ShapeDtypeStruct(late, BF16),
            jax.ShapeDtypeStruct((n,) + shard.shape, BF16),
        ],
        in_specs=[SMEM, VMEM, VMEM, VMEM, VMEM],
        out_specs=[VMEM] * 3,
        scratch_shapes=[
            pltpu.VMEM((width, 4 * width), F32),
            pltpu.VMEM((4 * width, width), BF16),
            pltpu.VMEM((devices * 3 * EARLY, 128), F32),
            pltpu.VMEM((devices * 16, 128), F32),
            pltpu.VMEM(early, BF16),
            pltpu.VMEM(late, BF16),
            pltpu.SemaphoreType.DMA((3,)),
            pltpu.SemaphoreType.DMA((3,)),
            pltpu.SemaphoreType.DMA((3,)),
        ],
        compiler_params=pltpu.CompilerParams(
            collective_id=1, has_side_effects=True, vmem_limit_bytes=50 * 2**20
        ),
        name="feature_attention",
    )(count, x, full, shard, gains_t)


def exchange(groups, devices, src_ref, dst_ref, send, recv, own_sem):
    fsdp, feat = lax.axis_index("fsdp"), lax.axis_index("feat")
    me = fsdp * groups + feat
    barrier = pltpu.get_barrier_semaphore()

    @pl.loop(1, devices)
    def _(k):
        pl.semaphore_signal(
            barrier, inc=1, device_id=position(fsdp, feat, k, groups, devices), device_id_type=MESH
        )

    own = pltpu.make_async_copy(src_ref.at[me], dst_ref.at[me], own_sem)
    own.start()
    pl.semaphore_wait(barrier, devices - 1)

    def copy(k):
        to = position(fsdp, feat, k, groups, devices)
        return pltpu.make_async_remote_copy(
            src_ref=src_ref.at[to[0] * groups + to[1]],
            dst_ref=dst_ref.at[me],
            send_sem=send,
            recv_sem=recv,
            device_id=to,
            device_id_type=MESH,
        )

    @pl.loop(1, devices)
    def _(k):
        copy(k).start()

    own.wait()
    wait_all(dst_ref, devices - 1, send)
    wait_all(dst_ref, devices - 1, recv)


def sample_kernel(
    block_q, block_k, count_ref, early_ref, late_ref, full_ref, gains_ref, out_ref,
    w_f32, w_ref, cells, x_t, q_all, k_all, v_all, acc, top, out_t,
):
    devices = early_ref.shape[0]
    total = cells.shape[1]
    rows = total // devices
    width = gains_ref.shape[0]
    head = width // HEADS
    scale = head**-0.5 * 1.4426950408889634
    stack_weights(full_ref, 0, 8 * width, w_f32, w_ref)

    def unpack(i, carry):
        for j in range(2):
            at = pl.multiple_of(i * 2 * rows, 8) + j * rows
            for ref, first, last in ((early_ref, 0, EARLY), (late_ref, EARLY, rows)):
                block = ref[2 * i + j].astype(F32)
                count = last - first
                for t in range(3):
                    cells[t, pl.ds(at + first, count), :] = block[t * count : (t + 1) * count]
        return carry

    lax.fori_loop(0, devices // 2, unpack, 0, unroll=2)
    for t in range(3):
        for c in range(0, total, 128):
            x_t[t * 128 : (t + 1) * 128, c : c + 128] = cells[t, c : c + 128, :].T
    gain2, gain3 = gains_ref[:, 1:2], gains_ref[:, 2:3]
    ones = first_row(block_q, 1.0).astype(BF16)
    live_blocks = lax.div(count_ref[0] + (block_k - 1), block_k)

    for f in range(2):
        base = f * width

        def project(b, carry):
            at = pl.multiple_of(b * block_q, 128)
            lanes = pl.ds(at, block_q)
            normed = norm_t(x_t[base : base + width, lanes], gain2)
            qkv = dot(w_ref[0 : 3 * width, :], normed)
            live = lax.broadcasted_iota(jnp.int32, (1, block_q), 1) + at < count_ref[0]
            mask = first_row(block_q, jnp.where(live, 0.0, NEGATIVE))
            for h in range(HEADS):
                q = (qkv[h * head : (h + 1) * head] * scale).astype(BF16)
                q_all[h, :, lanes] = jnp.concatenate([q, ones], axis=0)
                k = jnp.concatenate([qkv[width + h * head : width + (h + 1) * head], mask], axis=0)
                k_all[h, lanes, :] = k.T.astype(BF16)
                v = qkv[2 * width + h * head : 2 * width + (h + 1) * head].astype(BF16)
                v_all[h, :, lanes] = jnp.concatenate([v, ones], axis=0)
            return carry

        lax.fori_loop(0, total // block_q, project, 0)

        def queries(b, carry):
            lanes = pl.ds(pl.multiple_of(b * block_q, 128), block_q)
            acc[...] = jnp.zeros_like(acc)
            top[...] = jnp.full_like(top, NEGATIVE)

            def keys(j, inner):
                span = pl.ds(pl.multiple_of(j * block_k, 128), block_k)
                def score(h):
                    return dot(k_all[h, span, :], q_all[h, :, lanes])

                s = score(0)
                for h in range(HEADS):
                    following = score(h + 1) if h + 1 < HEADS else None
                    before = top[h : h + 1]
                    now = jnp.maximum(before, jnp.max(s, axis=0, keepdims=True))
                    p = jnp.exp2(s - now).astype(BF16)
                    top[h : h + 1] = now
                    acc[h] = acc[h] * jnp.exp2(before - now) + dot(v_all[h, :, span], p)
                    s = following
                return inner

            lax.fori_loop(0, live_blocks, keys, 0)
            heads = [(acc[h, :head] / acc[h, head : head + 1]).astype(BF16) for h in range(HEADS)]
            y = dot(w_ref[3 * width : 4 * width, :], jnp.concatenate(heads, axis=0))
            sampled = (y + x_t[base : base + width, lanes]).astype(BF16).astype(F32)
            normed = norm_t(sampled, gain3)
            hidden = jax.nn.gelu(dot(w_ref[4 * width : 6 * width, :], normed)).astype(BF16)
            y = dot(w_ref[6 * width : 7 * width, :], hidden[:width])
            y += dot(w_ref[7 * width : 8 * width, :], hidden[width:])
            out_t[base : base + width, lanes] = sampled + y
            return carry

        lax.fori_loop(0, total // block_q, queries, 0)

    for t in range(3):
        for c in range(0, total, 128):
            cells[t, c : c + 128, :] = out_t[t * 128 : (t + 1) * 128, c : c + 128].T

    def pack(i, carry):
        for j in range(2):
            at = pl.multiple_of(i * 2 * rows, 8)
            for t in range(3):
                out_ref[2 * i + j, t * rows : (t + 1) * rows, :] = cells[
                    t, pl.ds(at + j * rows, rows), :
                ].astype(BF16)
        return carry

    lax.fori_loop(0, devices // 2, pack, 0, unroll=2)


def sample_part(count, early, late, full, gains_t, total):
    width = gains_t.shape[0]
    devices = early.shape[0]
    block_q, block_k = 512, 384
    return pl.pallas_call(
        functools.partial(sample_kernel, block_q, block_k),
        out_shape=jax.ShapeDtypeStruct((devices, MSG, 128), BF16),
        in_specs=[SMEM, VMEM, VMEM, VMEM, VMEM],
        out_specs=VMEM,
        scratch_shapes=[
            pltpu.VMEM((width, 8 * width), F32),
            pltpu.VMEM((8 * width, width), BF16),
            pltpu.VMEM((3, total, 128), F32),
            pltpu.VMEM((2 * width, total), F32),
            pltpu.VMEM((HEADS, EXT, total), BF16),
            pltpu.VMEM((HEADS, total, EXT), BF16),
            pltpu.VMEM((HEADS, EXT, total), BF16),
            pltpu.VMEM((HEADS, EXT, block_q), F32),
            pltpu.VMEM((8, block_q), F32),
            pltpu.VMEM((2 * width, total), F32),
        ],
        compiler_params=pltpu.CompilerParams(vmem_limit_bytes=56 * 2**20),
        name="sample_attention",
    )(count, early, late, full, gains_t)


def back_kernel(groups, devices, src_ref, out_ref, landed, cells, send, recv, own_sem):
    rows, feats, width = out_ref.shape
    half = feats // 2
    exchange(groups, devices, src_ref, landed, send, recv, own_sem)

    def unpack(d, carry):
        cells[pl.ds(pl.multiple_of(d * MSG, 8), MSG), :] = landed[d].astype(F32)
        return carry

    lax.fori_loop(0, devices, unpack, 0, unroll=4)

    def row(r, carry):
        a, b, c = (cells[pl.ds(t * rows + r, half, stride=MSG), :] for t in range(3))
        out_ref[r, :half, :128] = a.astype(BF16)
        out_ref[r, :half, 128:] = b[:, :64].astype(BF16)
        out_ref[r, half:, :] = jnp.concatenate([b[:, 64:], c], axis=1).astype(BF16)
        return carry

    lax.fori_loop(0, rows, row, 0)


def back_to_rows(messages, groups, shape):
    devices = messages.shape[0]
    return pl.pallas_call(
        functools.partial(back_kernel, groups, devices),
        out_shape=jax.ShapeDtypeStruct(shape, BF16),
        in_specs=[VMEM],
        out_specs=VMEM,
        scratch_shapes=[
            pltpu.VMEM(messages.shape, BF16),
            pltpu.VMEM((devices * MSG, 128), F32),
            *[pltpu.SemaphoreType.DMA] * 3,
        ],
        compiler_params=pltpu.CompilerParams(
            collective_id=2, has_side_effects=True, vmem_limit_bytes=40 * 2**20
        ),
        name="back_to_rows",
    )(messages)


def local(table_cells, attn, up, down, norm_gains, train_count, feature_count):
    rows, feats, width = table_cells.shape
    n, groups = lax.axis_size("fsdp"), lax.axis_size("feat")
    devices = n * groups
    part = width // n
    attn = jnp.swapaxes(attn, 0, 1).reshape(part, 8 * width)
    rest = jnp.concatenate(
        [
            attn[:, 4 * width :],
            jnp.swapaxes(up.reshape(part, width, 2), 1, 2).reshape(part, 2 * width),
            down.reshape(part, 2 * width),
        ],
        axis=1,
    )
    full = gather(attn[:, : 4 * width], n)
    gains_t = norm_gains.T
    early, late, rest = feature_part(
        feature_count, table_cells, full, rest, gains_t, groups, devices
    )
    done = sample_part(train_count, early, late, rest, gains_t, rows * devices)
    return back_to_rows(done, groups, table_cells.shape)


def solution(mesh):
    in_specs = (
        P(("fsdp", "feat"), None, None),
        P(None, "fsdp", None),
        P("fsdp", None),
        P("fsdp", None),
        P(),
        P(),
        P(),
    )
    out_specs = P(("fsdp", "feat"), None, None)
    return jax.shard_map(local, mesh=mesh, in_specs=in_specs, out_specs=out_specs, check_vma=False)
```

```python
import functools

import jax
import jax.numpy as jnp
from jax import lax
from jax.experimental import pallas as pl
from jax.experimental.pallas import tpu as pltpu
from jax.sharding import PartitionSpec as P

MESH = pl.DeviceIdType.MESH
HEADS = 6
EPS = 1e-05
NEGATIVE = -1e30
EXT = 48
MSG = 40
EARLY = 8
F32 = jnp.float32
BF16 = jnp.bfloat16
VMEM = pl.BlockSpec(memory_space=pltpu.VMEM)
HBM = pl.BlockSpec(memory_space=pl.ANY)
SMEM = pl.BlockSpec(memory_space=pltpu.SMEM)


def norm_t(cells_t, gain):
    mean = jnp.mean(cells_t, axis=0, keepdims=True)
    centered = cells_t - mean
    var = jnp.mean(centered * centered, axis=0, keepdims=True)
    return (centered * lax.rsqrt(var + EPS) * gain).astype(BF16)


def dot(a, b):
    return jnp.dot(a, b, preferred_element_type=F32)


def first_row(count, top):
    rows = lax.broadcasted_iota(jnp.int32, (16, count), 0)
    return jnp.where(rows == 0, top, 0.0).astype(F32)


def wait_all(ref, count, sem):
    blocks = ref.at[pl.ds(0, count)]
    pltpu.make_async_copy(blocks, blocks, sem).wait()


def position(fsdp, feat, k, groups, devices):
    d = lax.rem(fsdp * groups + feat + k, devices)
    return d // groups, lax.rem(d, groups)


def layer_kernel(
    groups, devices, extent, block,
    x_hbm, attn_ref, up_ref, down_ref, gains_ref, train_ref, feat_ref, out_ref,
    x_ref, rest_f32, x_all, normed_all, first_shard, rest_shard, first_full, rest_full,
    w_f32, d_f32, w_one, w_two, w_down, cells_a, cells_b, out_a, out_b, early_ref, late_ref,
    cells, x_t, q_all, k_all, v_all, out_t, packed, landed, spread,
    w_send, w_recv, own, send, recv, back_send, back_recv,
):
    rows, feats, width = x_ref.shape
    head = width // HEADS
    half = feats // 2
    n = devices // groups
    part = width // n
    total = rows * devices
    scale = head**-0.5 * 1.4426950408889634
    fsdp, feat = lax.axis_index("fsdp"), lax.axis_index("feat")
    me = fsdp * groups + feat

    fetch = pltpu.make_async_copy(x_hbm, x_ref, own.at[0])
    fetch.start()
    barrier = pltpu.get_barrier_semaphore()

    @pl.loop(1, devices)
    def _(k):
        pl.semaphore_signal(
            barrier, inc=1, device_id=position(fsdp, feat, k, groups, devices), device_id_type=MESH
        )

    def beside(*parts):
        return jnp.concatenate([v.astype(F32) for v in parts], axis=1).astype(BF16)

    first_shard[...] = beside(*(attn_ref[i] for i in range(4)))
    rest_shard[...] = beside(
        *(attn_ref[i] for i in range(4, 8)), up_ref[...], down_ref[:part], down_ref[part:]
    )
    own_first = pltpu.make_async_copy(first_shard, first_full.at[fsdp], own.at[1])
    own_first.start()
    own_rest = pltpu.make_async_copy(rest_shard, rest_full.at[fsdp], own.at[2])
    own_rest.start()
    gains_t = jnp.concatenate([gains_ref[...], jnp.zeros((5, width), F32)], axis=0).T
    gain1, gain2, gain3 = (gains_t[:, i : i + 1] for i in range(3))

    def send_shard(k, src, dst, which):
        pltpu.make_async_remote_copy(
            src_ref=src, dst_ref=dst.at[fsdp], send_sem=w_send.at[which], recv_sem=w_recv.at[which],
            device_id=(lax.rem(fsdp + k, n), feat), device_id_type=MESH,
        ).start()

    pl.semaphore_wait(barrier, devices - 1)

    @pl.loop(1, n)
    def _(k):
        send_shard(k, first_shard, first_full, 0)

    fetch.wait()

    @pl.loop(0, rows // 2)
    def _(i):
        cells_t = jnp.concatenate([x_ref[2 * i + j].astype(F32).T for j in range(2)], axis=1)
        x_all[i] = cells_t
        normed_all[i] = norm_t(cells_t, gain1)

    own_first.wait()
    wait_all(first_full, n - 1, w_recv.at[0])

    @pl.loop(1, n)
    def _(k):
        send_shard(k, rest_shard, rest_full, 1)

    for i in range(n):
        w_f32[pl.ds(i * part, part), :] = first_full[i].astype(F32)
    for c in range(0, 4 * width, 128):
        w_one[c : c + 128, :] = w_f32[:, c : c + 128].T.astype(BF16)

    live = lax.broadcasted_iota(jnp.int32, (1, feats), 1) < feat_ref[0]
    mask = first_row(feats, jnp.where(live, 0.0, NEGATIVE))
    ones_b = first_row(feats, 1.0).astype(BF16)

    def two_rows(i, into, stride, height, skip):
        qkv = dot(w_one[0 : 3 * width, :], normed_all[i])

        def piece(unit, kind):
            j, h = unit // HEADS, unit % HEADS
            at = kind * width + h * head
            return qkv[at : at + head, j * feats : (j + 1) * feats]

        def score(unit):
            q = jnp.concatenate([(piece(unit, 0) * scale).astype(BF16), ones_b], axis=0)
            k = jnp.concatenate([piece(unit, 1), mask], axis=0).T.astype(BF16)
            return dot(k, q)

        heads = []
        s = score(0)
        for unit in range(2 * HEADS):
            following = score(unit + 1) if unit + 1 < 2 * HEADS else None
            p = jnp.exp2(s - jnp.max(s, axis=0, keepdims=True)).astype(BF16)
            o = dot(jnp.concatenate([piece(unit, 2).astype(BF16), ones_b], axis=0), p)
            heads.append((o[:head] / o[head : head + 1]).astype(BF16))
            s = following
        heads = jnp.concatenate(
            [jnp.concatenate(heads[:HEADS], axis=0), jnp.concatenate(heads[HEADS:], axis=0)], axis=1
        )
        y = dot(w_one[3 * width : 4 * width, :], heads) + x_all[i]
        for j in range(2):
            at = j * feats
            m = jnp.concatenate([y[:, at : at + half], y[:, at + half : at + feats]], axis=0)
            for t in range(3):
                into[pl.ds(t * height + 2 * i + j - skip, half, stride=stride), :] = m[
                    t * 128 : (t + 1) * 128
                ].T

    def pack(source, out, d):
        stride = source.shape[0] // devices
        at = pl.multiple_of(d * stride, 8)
        out[d] = source[pl.ds(at, out.shape[1]), :].astype(BF16)

    def send_cells(k, src, dst, which):
        to = position(fsdp, feat, k, groups, devices)
        pltpu.make_async_remote_copy(
            src_ref=src.at[to[0] * groups + to[1]], dst_ref=dst.at[me],
            send_sem=send.at[which], recv_sem=recv.at[which],
            device_id=to, device_id_type=MESH,
        ).start()

    @pl.loop(0, EARLY // 2)
    def _(i):
        two_rows(i, cells_a, 3 * EARLY, EARLY, 0)

    pack(cells_a, out_a, me)
    own_a = pltpu.make_async_copy(out_a.at[me], early_ref.at[me], own.at[3])
    own_a.start()

    @pl.loop(1, devices)
    def _(k):
        pack(cells_a, out_a, lax.rem(me + k, devices))
        send_cells(k, out_a, early_ref, 0)

    @pl.loop(EARLY // 2, rows // 2)
    def _(i):
        two_rows(i, cells_b, 16, rows - EARLY, EARLY)

    pack(cells_b, out_b, me)
    own_b = pltpu.make_async_copy(out_b.at[me], late_ref.at[me], own.at[4])
    own_b.start()

    @pl.loop(1, devices)
    def _(k):
        pack(cells_b, out_b, lax.rem(me + k, devices))
        send_cells(k, out_b, late_ref, 1)

    own_rest.wait()
    wait_all(rest_full, n - 1, w_recv.at[1])
    down_at = 6 * width
    for i in range(n):
        shard = rest_full[i].astype(F32)
        rest_f32[pl.ds(i * part, part), :] = shard[:, :down_at]
        for j in range(2):
            at = down_at + j * width
            d_f32[pl.ds((2 * i + j) * part, part), :] = shard[:, at : at + width]
    for c in range(0, down_at, 128):
        w_two[c : c + 128, :] = rest_f32[:, c : c + 128].T.astype(BF16)
    w_down[...] = d_f32[...].T.astype(BF16)

    def unpack(ref, first, last):
        count = last - first

        @pl.loop(0, devices // 2, unroll=2)
        def _(i):
            for j in range(2):
                received = ref[2 * i + j].astype(F32)
                at = pl.multiple_of(i * 2 * rows, 8) + j * rows + first
                for t in range(3):
                    cells[t, pl.ds(at, count), :] = received[t * count : (t + 1) * count]

    own_a.wait()
    wait_all(early_ref, devices - 1, recv.at[0])
    unpack(early_ref, 0, EARLY)
    own_b.wait()
    wait_all(late_ref, devices - 1, recv.at[1])
    unpack(late_ref, EARLY, rows)

    blocks = total // block
    peers = devices // blocks
    plane, place = me // peers, lax.rem(me, peers)
    for t in range(3):
        for c in range(0, total, 128):
            x_t[t * 128 : (t + 1) * 128, c : c + 128] = cells[t, c : c + 128, :].T
    ones = first_row(block, 1.0).astype(BF16)

    def project(step, with_keys):
        f, b = lax.rem(step, 2), step // 2
        at = pl.multiple_of(b * block, 128)
        lanes = pl.ds(at, block)
        base = pl.multiple_of(f * width, 8)
        normed = norm_t(x_t[pl.ds(base, width), lanes], gain2)
        qkv = dot(w_two[0 : (3 if with_keys else 1) * width, :], normed)
        live = lax.broadcasted_iota(jnp.int32, (1, block), 1) + at < train_ref[0]
        mask = first_row(block, jnp.where(live, 0.0, NEGATIVE))
        for h in range(HEADS):
            q = (qkv[h * head : (h + 1) * head] * scale).astype(BF16)
            q_all[f, h, :, lanes] = jnp.concatenate([q, ones], axis=0)
            if with_keys:
                k = jnp.concatenate([qkv[width + h * head : width + (h + 1) * head], mask], axis=0)
                k_all[f, h, lanes, :] = k.T.astype(BF16)
                v = qkv[2 * width + h * head : 2 * width + (h + 1) * head].astype(BF16)
                v_all[f, h, :, lanes] = jnp.concatenate([v, ones], axis=0)

    key_blocks = -(-extent // block)

    @pl.loop(0, 2 * key_blocks)
    def _(step):
        project(step, True)

    @pl.loop(2 * key_blocks, 2 * blocks)
    def _(step):
        project(step, False)

    def attend(b, f):
        lanes = pl.ds(pl.multiple_of(b * block, 128), block)
        base = pl.multiple_of(f * width, 8)

        def score(h):
            return dot(k_all[f, h, :extent, :], q_all[f, h, :, lanes])

        heads = []
        s = score(0)
        for h in range(HEADS):
            following = score(h + 1) if h + 1 < HEADS else None
            p = jnp.exp2(s - jnp.max(s, axis=0, keepdims=True)).astype(BF16)
            o = dot(v_all[f, h, :, :extent], p)
            heads.append((o[:head] / o[head : head + 1]).astype(BF16))
            s = following
        y = dot(w_two[3 * width : 4 * width, :], jnp.concatenate(heads, axis=0))
        sampled = (y + x_t[pl.ds(base, width), lanes]).astype(BF16).astype(F32)
        normed = norm_t(sampled, gain3)
        hidden = jax.nn.gelu(dot(w_two[4 * width : 6 * width, :], normed)).astype(BF16)
        out_t[pl.ds(base, width), :] = sampled + dot(w_down[...], hidden)

    def prepare(b):
        @pl.loop(0, 2)
        def _(f):
            attend(b, f)

        for t in range(3):
            for c in range(0, block, 128):
                cells[t, c : c + 128, :] = out_t[t * 128 : (t + 1) * 128, c : c + 128].T

        @pl.loop(0, peers // 2)
        def _(i):
            for j in range(2):
                at = pl.multiple_of(i * 2 * rows, 8) + j * rows
                for t in range(3):
                    packed[b * peers + 2 * i + j, t * rows : (t + 1) * rows, :] = cells[
                        t, pl.ds(at, rows), :
                    ].astype(BF16)

    def send_back(b, k, which):
        to = b * peers + lax.rem(place + k, peers)
        pltpu.make_async_remote_copy(
            src_ref=packed.at[to], dst_ref=landed.at[me],
            send_sem=back_send.at[which], recv_sem=back_recv.at[which],
            device_id=(to // groups, lax.rem(to, groups)), device_id_type=MESH,
        ).start()

    def place_group(source, count, which):
        wait_all(landed, count, back_recv.at[which])
        base = source * peers

        @pl.loop(0, peers, unroll=4)
        def _(d):
            spread[pl.ds(pl.multiple_of(d * MSG, 8), 3 * rows), :] = landed[base + d].astype(F32)

        low = pl.ds(pl.multiple_of(base, 16), peers)
        high = pl.ds(pl.multiple_of(half + base, 16), peers)

        @pl.loop(0, rows)
        def _(r):
            u, v, w = (spread[pl.ds(t * rows + r, peers, stride=MSG), :] for t in range(3))
            out_ref[r, low, :] = jnp.concatenate([u, v[:, :64]], axis=1).astype(BF16)
            out_ref[r, high, :] = jnp.concatenate([v[:, 64:], w], axis=1).astype(BF16)

    order = [blocks // 2] + [i for i in range(1, blocks) if i != blocks // 2] + [0]
    last = len(order) - 1
    for which, shift in enumerate(order[:-1]):
        b = lax.rem(plane + shift, blocks)
        prepare(b)

        @pl.loop(0, peers)
        def _(k):
            send_back(b, k, which)

    prepare(plane)
    own_back = pltpu.make_async_copy(packed.at[me], landed.at[me], own.at[5])
    own_back.start()

    @pl.loop(1, peers)
    def _(k):
        send_back(plane, k, last)

    for which, shift in enumerate(order[:-1]):
        place_group(lax.rem(plane + blocks - shift, blocks), peers, which)
    own_back.wait()
    place_group(plane, peers - 1, last)

    wait_all(first_full, n - 1, w_send.at[0])
    wait_all(rest_full, n - 1, w_send.at[1])
    wait_all(early_ref, devices - 1, send.at[0])
    wait_all(late_ref, devices - 1, send.at[1])
    for which in range(len(order)):
        wait_all(packed, peers if which < last else peers - 1, back_send.at[which])


def local(table_cells, attn, up, down, norm_gains, train_count, feature_count):
    rows, feats, width = table_cells.shape
    n, groups = lax.axis_size("fsdp"), lax.axis_size("feat")
    devices = n * groups
    part = width // n
    total = rows * devices
    blocks = 4
    block = total // blocks
    extent = total * 3 // 4
    early, late = (devices, 3 * EARLY, 128), (devices, 3 * (rows - EARLY), 128)
    message = (devices, 3 * rows, 128)
    vmem = pltpu.VMEM
    return pl.pallas_call(
        functools.partial(layer_kernel, groups, devices, extent, block),
        out_shape=jax.ShapeDtypeStruct(table_cells.shape, BF16),
        in_specs=[HBM, VMEM, VMEM, VMEM, VMEM, SMEM, SMEM],
        out_specs=VMEM,
        scratch_shapes=[
            vmem(table_cells.shape, BF16),
            vmem((width, 6 * width), F32),
            vmem((rows // 2, width, 2 * feats), F32),
            vmem((rows // 2, width, 2 * feats), BF16),
            vmem((part, 4 * width), BF16),
            vmem((part, 8 * width), BF16),
            vmem((n, part, 4 * width), BF16),
            vmem((n, part, 8 * width), BF16),
            vmem((width, 4 * width), F32),
            vmem((2 * width, width), F32),
            vmem((4 * width, width), BF16),
            vmem((6 * width, width), BF16),
            vmem((width, 2 * width), BF16),
            vmem((devices * 3 * EARLY, 128), F32),
            vmem((devices * 16, 128), F32),
            vmem(early, BF16),
            vmem(late, BF16),
            vmem(early, BF16),
            vmem(late, BF16),
            vmem((3, total, 128), F32),
            vmem((2 * width, total), F32),
            vmem((2, HEADS, EXT, total), BF16),
            vmem((2, HEADS, total, EXT), BF16),
            vmem((2, HEADS, EXT, total), BF16),
            vmem((2 * width, block), F32),
            vmem(message, BF16),
            vmem(message, BF16),
            vmem((devices // blocks * MSG, 128), F32),
            pltpu.SemaphoreType.DMA((2,)),
            pltpu.SemaphoreType.DMA((2,)),
            pltpu.SemaphoreType.DMA((6,)),
            pltpu.SemaphoreType.DMA((2,)),
            pltpu.SemaphoreType.DMA((2,)),
            pltpu.SemaphoreType.DMA((blocks,)),
            pltpu.SemaphoreType.DMA((blocks,)),
        ],
        compiler_params=pltpu.CompilerParams(
            collective_id=0, has_side_effects=True, vmem_limit_bytes=56 * 2**20
        ),
        name="layer",
    )(table_cells, attn, up, down, norm_gains, train_count, feature_count)


def solution(mesh):
    in_specs = (
        P(("fsdp", "feat"), None, None),
        P(None, "fsdp", None),
        P("fsdp", None),
        P("fsdp", None),
        P(),
        P(),
        P(),
    )
    out_specs = P(("fsdp", "feat"), None, None)
    return jax.shard_map(local, mesh=mesh, in_specs=in_specs, out_specs=out_specs, check_vma=False)
```

```python
import functools

import jax
import jax.numpy as jnp
from jax import lax
from jax.experimental import pallas as pl
from jax.experimental.pallas import tpu as pltpu
from jax.sharding import PartitionSpec as P

MESH = pl.DeviceIdType.MESH
HEADS = 6
EPS = 1e-05
NEGATIVE = -1e30
EXT = 48
MSG = 40
EARLY = 8
F32 = jnp.float32
BF16 = jnp.bfloat16
VMEM = pl.BlockSpec(memory_space=pltpu.VMEM)
HBM = pl.BlockSpec(memory_space=pl.ANY)
SMEM = pl.BlockSpec(memory_space=pltpu.SMEM)


def norm_t(cells_t, gain):
    mean = jnp.mean(cells_t, axis=0, keepdims=True)
    centered = cells_t - mean
    var = jnp.mean(centered * centered, axis=0, keepdims=True)
    return (centered * lax.rsqrt(var + EPS) * gain).astype(BF16)


def dot(a, b):
    return jnp.dot(a, b, preferred_element_type=F32)


def first_row(count, top):
    rows = lax.broadcasted_iota(jnp.int32, (16, count), 0)
    return jnp.where(rows == 0, top, 0.0).astype(F32)


def wait_all(ref, count, sem):
    blocks = ref.at[pl.ds(0, count)]
    pltpu.make_async_copy(blocks, blocks, sem).wait()


def loop(first, last, body, unroll=8):
    whole = (last - first) // unroll

    @pl.loop(0, whole)
    def _(i):
        for j in range(unroll):
            body(first + i * unroll + j)

    for k in range(first + whole * unroll, last):
        body(k)


def position(fsdp, feat, k, groups, devices):
    d = lax.rem(fsdp * groups + feat + k, devices)
    return d // groups, lax.rem(d, groups)


def layer_kernel(
    groups, devices, extent, block,
    x_hbm, attn_ref, up_ref, down_ref, gains_ref, train_ref, feat_ref, out_ref,
    x_ref, rest_f32, x_all, normed_all, first_shard, rest_shard, first_full, rest_full,
    w_f32, d_f32, w_one, w_two, w_down, cells_a, cells_b, out_a, out_b, early_ref, late_ref,
    cells, x_t, q_all, k_all, v_all, out_t, packed, landed, spread,
    w_send, w_recv, own, send, recv, back_send, back_recv,
):
    rows, width, feats = x_ref.shape
    head = width // HEADS
    half = feats // 2
    n = devices // groups
    part = width // n
    total = rows * devices
    scale = head**-0.5 * 1.4426950408889634
    fsdp, feat = lax.axis_index("fsdp"), lax.axis_index("feat")
    me = fsdp * groups + feat
    chip, core = fsdp // 2, lax.rem(fsdp, 2)
    chips = n // 2

    fetch = pltpu.make_async_copy(x_hbm, x_ref, own.at[0])
    fetch.start()
    barrier = pltpu.get_barrier_semaphore()

    def greet(k):
        pl.semaphore_signal(
            barrier, inc=1, device_id=position(fsdp, feat, k, groups, devices), device_id_type=MESH
        )

    loop(1, devices, greet)

    def beside(*parts):
        return jnp.concatenate([v.astype(F32) for v in parts], axis=1).astype(BF16)

    first_shard[...] = beside(*(attn_ref[:, i] for i in range(4)))
    rest_shard[...] = beside(
        *(attn_ref[:, i] for i in range(4, 8)), up_ref[...], down_ref[:part], down_ref[part:]
    )
    own_first = pltpu.make_async_copy(first_shard, first_full.at[core, chip], own.at[1])
    own_first.start()
    own_rest = pltpu.make_async_copy(rest_shard, rest_full.at[core, chip], own.at[2])
    own_rest.start()
    gains_t = jnp.concatenate([gains_ref[...], jnp.zeros((5, width), F32)], axis=0).T
    gain1, gain2, gain3 = (gains_t[:, i : i + 1] for i in range(3))

    def send_shard(k, src, dst, which):
        pltpu.make_async_remote_copy(
            src_ref=src, dst_ref=dst.at[core, chip],
            send_sem=w_send.at[which], recv_sem=w_recv.at[which],
            device_id=(lax.rem(chip + k, chips) * 2 + core, feat), device_id_type=MESH,
        ).start()

    def to_neighbour(full, which):
        return pltpu.make_async_remote_copy(
            src_ref=full.at[core], dst_ref=full.at[core],
            send_sem=w_send.at[which], recv_sem=w_recv.at[which],
            device_id=(chip * 2 + 1 - core, feat), device_id_type=MESH,
        )

    pl.semaphore_wait(barrier, devices - 1)

    loop(1, chips, lambda k: send_shard(k, first_shard, first_full, 0))

    fetch.wait()

    @pl.loop(0, rows // 2)
    def _(i):
        cells_t = jnp.concatenate([x_ref[2 * i + j].astype(F32) for j in range(2)], axis=1)
        x_all[i] = cells_t
        normed_all[i] = norm_t(cells_t, gain1)

    own_first.wait()
    wait_all(first_full.at[0], chips - 1, w_recv.at[0])
    first_pair = to_neighbour(first_full, 1)
    first_pair.start()
    first_pair.wait()

    for i in range(n):
        w_f32[pl.ds(i * part, part), :] = first_full[i % 2, i // 2].astype(F32)
        if 0 < i < chips:
            send_shard(i, rest_shard, rest_full, 2)
    for c in range(0, 4 * width, 128):
        w_one[c : c + 128, :] = w_f32[:, c : c + 128].T.astype(BF16)

    live = lax.broadcasted_iota(jnp.int32, (1, feats), 1) < feat_ref[0]
    mask = first_row(feats, jnp.where(live, 0.0, NEGATIVE))
    ones_b = first_row(feats, 1.0).astype(BF16)

    def two_rows(i, into, stride, height, skip):
        qkv = dot(w_one[0 : 3 * width, :], normed_all[i])

        def piece(unit, kind):
            j, h = unit // HEADS, unit % HEADS
            at = kind * width + h * head
            return qkv[at : at + head, j * feats : (j + 1) * feats]

        def score(unit):
            q = jnp.concatenate([(piece(unit, 0) * scale).astype(BF16), ones_b], axis=0)
            k = jnp.concatenate([piece(unit, 1), mask], axis=0).T.astype(BF16)
            return dot(k, q)

        heads = []
        s = score(0)
        for unit in range(2 * HEADS):
            following = score(unit + 1) if unit + 1 < 2 * HEADS else None
            p = jnp.exp2(s - jnp.max(s, axis=0, keepdims=True)).astype(BF16)
            o = dot(jnp.concatenate([piece(unit, 2).astype(BF16), ones_b], axis=0), p)
            heads.append((o[:head] / o[head : head + 1]).astype(BF16))
            s = following
        heads = jnp.concatenate(
            [jnp.concatenate(heads[:HEADS], axis=0), jnp.concatenate(heads[HEADS:], axis=0)], axis=1
        )
        y = dot(w_one[3 * width : 4 * width, :], heads) + x_all[i]
        for j in range(2):
            at = j * feats
            m = jnp.concatenate([y[:, at : at + half], y[:, at + half : at + feats]], axis=0)
            for t in range(3):
                into[pl.ds(t * height + 2 * i + j - skip, half, stride=stride), :] = m[
                    t * 128 : (t + 1) * 128
                ].T

    def pack(source, out, d):
        stride = source.shape[0] // devices
        at = pl.multiple_of(d * stride, 8)
        out[d] = source[pl.ds(at, out.shape[1]), :].astype(BF16)

    def send_cells(k, src, dst, which):
        to = position(fsdp, feat, k, groups, devices)
        pltpu.make_async_remote_copy(
            src_ref=src.at[to[0] * groups + to[1]], dst_ref=dst.at[me],
            send_sem=send.at[which], recv_sem=recv.at[which],
            device_id=to, device_id_type=MESH,
        ).start()

    @pl.loop(0, EARLY // 2)
    def _(i):
        two_rows(i, cells_a, 3 * EARLY, EARLY, 0)

    own_rest.wait()
    wait_all(rest_full.at[0], chips - 1, w_recv.at[2])
    rest_pair = to_neighbour(rest_full, 3)
    rest_pair.start()
    pack(cells_a, out_a, me)
    own_a = pltpu.make_async_copy(out_a.at[me], early_ref.at[me], own.at[3])
    own_a.start()

    def send_early(k):
        pack(cells_a, out_a, lax.rem(me + k, devices))
        send_cells(k, out_a, early_ref, 0)

    late_steps = (rows - EARLY) // 2
    beside_step = (devices - 1) // late_steps
    for k in range(1 + late_steps * beside_step, devices):
        send_early(k)

    @pl.loop(0, late_steps)
    def _(i):
        for k in range(beside_step):
            send_early(1 + i * beside_step + k)
        two_rows(EARLY // 2 + i, cells_b, 16, rows - EARLY, EARLY)

    pack(cells_b, out_b, me)
    own_b = pltpu.make_async_copy(out_b.at[me], late_ref.at[me], own.at[4])
    own_b.start()

    def send_late(k):
        pack(cells_b, out_b, lax.rem(me + k, devices))
        send_cells(k, out_b, late_ref, 1)

    rest_pair.wait()
    down_at = 6 * width
    for i in range(n):
        shard = rest_full[i % 2, i // 2].astype(F32)
        rest_f32[pl.ds(i * part, part), :] = shard[:, :down_at]
        for j in range(2):
            at = down_at + j * width
            d_f32[pl.ds((2 * i + j) * part, part), :] = shard[:, at : at + width]
        for k in range(max(1, i * groups), (i + 1) * groups):
            send_late(k)
    for c in range(0, down_at, 128):
        w_two[c : c + 128, :] = rest_f32[:, c : c + 128].T.astype(BF16)
    w_down[...] = d_f32[...].T.astype(BF16)

    def unpack(ref, first, last):
        count = last - first

        @pl.loop(0, devices // 2, unroll=8)
        def _(i):
            for j in range(2):
                received = ref[2 * i + j].astype(F32)
                at = pl.multiple_of(i * 2 * rows, 8) + j * rows + first
                for t in range(3):
                    cells[t, pl.ds(at, count), :] = received[t * count : (t + 1) * count]

    own_a.wait()
    wait_all(early_ref, devices - 1, recv.at[0])
    unpack(early_ref, 0, EARLY)
    own_b.wait()
    wait_all(late_ref, devices - 1, recv.at[1])
    unpack(late_ref, EARLY, rows)

    blocks = total // block
    peers = devices // blocks
    plane, place = me // peers, lax.rem(me, peers)
    for t in range(3):
        for c in range(0, total, 128):
            x_t[t * 128 : (t + 1) * 128, c : c + 128] = cells[t, c : c + 128, :].T
    ones = first_row(block, 1.0).astype(BF16)

    def project(step, with_keys):
        f, b = lax.rem(step, 2), step // 2
        at = pl.multiple_of(b * block, 128)
        lanes = pl.ds(at, block)
        base = pl.multiple_of(f * width, 8)
        normed = norm_t(x_t[pl.ds(base, width), lanes], gain2)
        qkv = dot(w_two[0 : (3 if with_keys else 1) * width, :], normed)
        live = lax.broadcasted_iota(jnp.int32, (1, block), 1) + at < train_ref[0]
        mask = first_row(block, jnp.where(live, 0.0, NEGATIVE))
        for h in range(HEADS):
            q = (qkv[h * head : (h + 1) * head] * scale).astype(BF16)
            q_all[f, h, :, lanes] = jnp.concatenate([q, ones], axis=0)
            if with_keys:
                k = jnp.concatenate([qkv[width + h * head : width + (h + 1) * head], mask], axis=0)
                k_all[f, h, lanes, :] = k.T.astype(BF16)
                v = qkv[2 * width + h * head : 2 * width + (h + 1) * head].astype(BF16)
                v_all[f, h, :, lanes] = jnp.concatenate([v, ones], axis=0)

    key_blocks = -(-extent // block)

    @pl.loop(0, 2 * key_blocks)
    def _(step):
        project(step, True)

    @pl.loop(2 * key_blocks, 2 * blocks)
    def _(step):
        project(step, False)

    def attend(b):
        lanes = pl.ds(pl.multiple_of(b * block, 128), block)

        def score(unit):
            f, h = unit // HEADS, unit % HEADS
            return dot(k_all[f, h, :extent, :], q_all[f, h, :, lanes])

        heads = []
        s = score(0)
        for unit in range(2 * HEADS):
            f, h = unit // HEADS, unit % HEADS
            following = score(unit + 1) if unit + 1 < 2 * HEADS else None
            p = jnp.exp2(s - jnp.max(s, axis=0, keepdims=True)).astype(BF16)
            o = dot(v_all[f, h, :, :extent], p)
            heads.append((o[:head] / o[head : head + 1]).astype(BF16))
            s = following
            if h + 1 < HEADS:
                continue
            base = f * width
            y = dot(w_two[3 * width : 4 * width, :], jnp.concatenate(heads, axis=0))
            heads = []
            sampled = (y + x_t[base : base + width, lanes]).astype(BF16).astype(F32)
            normed = norm_t(sampled, gain3)
            hidden = jax.nn.gelu(dot(w_two[4 * width : 6 * width, :], normed)).astype(BF16)
            out_t[base : base + width, :] = sampled + dot(w_down[...], hidden)

    def pack_back(b):
        for t in range(3):
            for c in range(0, block, 128):
                cells[t, c : c + 128, :] = out_t[t * 128 : (t + 1) * 128, c : c + 128].T

        @pl.loop(0, peers // 2, unroll=8)
        def _(i):
            for j in range(2):
                at = pl.multiple_of(i * 2 * rows, 8) + j * rows
                for t in range(3):
                    packed[b * peers + 2 * i + j, t * rows : (t + 1) * rows, :] = cells[
                        t, pl.ds(at, rows), :
                    ].astype(BF16)

    def send_back(b, k, which):
        to = b * peers + lax.rem(place + k, peers)
        pltpu.make_async_remote_copy(
            src_ref=packed.at[to], dst_ref=landed.at[me],
            send_sem=back_send.at[which], recv_sem=back_recv.at[which],
            device_id=(to // groups, lax.rem(to, groups)), device_id_type=MESH,
        ).start()

    def spread_group(source, count, which):
        wait_all(landed, count, back_recv.at[which])

        @pl.loop(0, peers, unroll=8)
        def _(i):
            d = source * peers + i
            spread[pl.ds(pl.multiple_of(d * MSG, 8), 3 * rows), :] = landed[d].astype(F32)

    last = blocks - 1

    def target(which):
        return lax.rem(plane + last - which, blocks)

    attend(target(0))

    pack_back(target(0))

    @pl.loop(1, blocks)
    def _(which):
        for k in range(peers):
            send_back(target(which - 1), k, which - 1)
        attend(target(which))

        pack_back(target(which))

    own_back = pltpu.make_async_copy(packed.at[me], landed.at[me], own.at[5])
    own_back.start()
    loop(1, peers, lambda k: send_back(plane, k, last))

    for which in range(last):
        spread_group(lax.rem(plane + 1 + which, blocks), peers, which)
    own_back.wait()
    spread_group(plane, peers - 1, last)

    @pl.loop(0, rows)
    def _(r):
        y = jnp.concatenate(
            [spread[pl.ds(t * rows + r, half, stride=MSG), :].T for t in range(3)], axis=0
        ).astype(BF16)
        out_ref[r, :, :half] = y[:width]
        out_ref[r, :, half:] = y[width:]


    wait_all(first_full.at[0], chips - 1, w_send.at[0])
    wait_all(rest_full.at[0], chips - 1, w_send.at[2])
    wait_all(early_ref, devices - 1, send.at[0])
    wait_all(late_ref, devices - 1, send.at[1])
    for which in range(blocks):
        wait_all(packed, peers if which < last else peers - 1, back_send.at[which])


def local(table_cells, attn, up, down, norm_gains, train_count, feature_count):
    table_t, attn = jnp.swapaxes(table_cells, 1, 2), jnp.swapaxes(attn, 0, 1)
    rows, width, feats = table_t.shape
    n, groups = lax.axis_size("fsdp"), lax.axis_size("feat")
    devices = n * groups
    part = width // n
    total = rows * devices
    blocks = 4
    block = total // blocks
    extent = total * 3 // 4
    early, late = (devices, 3 * EARLY, 128), (devices, 3 * (rows - EARLY), 128)
    message = (devices, 3 * rows, 128)
    vmem = pltpu.VMEM
    layer_t = pl.pallas_call(
        functools.partial(layer_kernel, groups, devices, extent, block),
        out_shape=jax.ShapeDtypeStruct(table_t.shape, BF16),
        in_specs=[HBM, VMEM, VMEM, VMEM, VMEM, SMEM, SMEM],
        out_specs=VMEM,
        scratch_shapes=[
            vmem(table_t.shape, BF16),
            vmem((width, 6 * width), F32),
            vmem((rows // 2, width, 2 * feats), F32),
            vmem((rows // 2, width, 2 * feats), BF16),
            vmem((part, 4 * width), BF16),
            vmem((part, 8 * width), BF16),
            vmem((2, n // 2, part, 4 * width), BF16),
            vmem((2, n // 2, part, 8 * width), BF16),
            vmem((width, 4 * width), F32),
            vmem((2 * width, width), F32),
            vmem((4 * width, width), BF16),
            vmem((6 * width, width), BF16),
            vmem((width, 2 * width), BF16),
            vmem((devices * 3 * EARLY, 128), F32),
            vmem((devices * 16, 128), F32),
            vmem(early, BF16),
            vmem(late, BF16),
            vmem(early, BF16),
            vmem(late, BF16),
            vmem((3, total, 128), F32),
            vmem((2 * width, total), F32),
            vmem((2, HEADS, EXT, total), BF16),
            vmem((2, HEADS, total, EXT), BF16),
            vmem((2, HEADS, EXT, total), BF16),
            vmem((2 * width, block), F32),
            vmem(message, BF16),
            vmem(message, BF16),
            vmem((devices * MSG, 128), F32),
            pltpu.SemaphoreType.DMA((4,)),
            pltpu.SemaphoreType.DMA((4,)),
            pltpu.SemaphoreType.DMA((6,)),
            pltpu.SemaphoreType.DMA((2,)),
            pltpu.SemaphoreType.DMA((2,)),
            pltpu.SemaphoreType.DMA((blocks,)),
            pltpu.SemaphoreType.DMA((blocks,)),
        ],
        compiler_params=pltpu.CompilerParams(
            collective_id=0, has_side_effects=True, vmem_limit_bytes=56 * 2**20
        ),
        name="layer",
    )(table_t, attn, up, down, norm_gains, train_count, feature_count)
    return jnp.swapaxes(layer_t, 1, 2)


def solution(mesh):
    in_specs = (
        P(("fsdp", "feat"), None, None),
        P(None, "fsdp", None),
        P("fsdp", None),
        P("fsdp", None),
        P(),
        P(),
        P(),
    )
    out_specs = P(("fsdp", "feat"), None, None)
    return jax.shard_map(local, mesh=mesh, in_specs=in_specs, out_specs=out_specs, check_vma=False)
```
